32 devices in a mesh: row: 8 (over z, y), col: 4 (over x, core).
Axes of the slice: x: 2, y: 2, z: 4, core: 2. Of those that a mesh axis runs over, the one named last changes fastest.
Arguments:
- amplitudes: float32 [16, 16, 400, 400], P('row', None, 'col'), may hold values from -6 to 6
- integrals: float32 [32, 32, 400, 400], P('row', None, 'col'), may hold values from -0.015625 to 0.015625
- rest: float32 [16, 16, 32, 32], P('col', None, 'row'), may hold values from -6 to 6
- occ_energy: float32 [16], replicated, may hold values from -2 to -0.5
- vir_energy: float32 [32], replicated, may hold values from 0.5 to 3
Outputs:
- new_amps: float32 [16, 16, 32, 32], P('col', None, 'row')
The draws below stay inside these ranges and needn't reach their ends.
All inputs are finite; a program needn't handle non-finite values.
Results may differ from the reference program's by a relative error of at most 0.000057.
Values sent between devices are 32-bit elements; how exact they have to be, the bound alone decides.
A program may use at most 128 MiB of HBM per device.

```python
import jax
import jax.numpy as jnp
from jax import lax

NV = 400
NO = 16
W = 32


def block_levels(rng, shape, pieces, least, top_value):
    factor_of, own = 1.0, jax.random.fold_in(rng, 6)
    for axis_at, parts in pieces:
        steps = jnp.exp(jax.random.uniform(jax.random.fold_in(own, axis_at), (parts,), jnp.float32, least / len(pieces), top_value / len(pieces)))
        factor_of = factor_of * jnp.repeat(steps, shape[axis_at] // parts).reshape([-1 if axis == axis_at else 1 for axis in range(len(shape))])
    return factor_of


def bell_draw(stream_key, dims, deviation, bound, cuts=(), held_as=jnp.bfloat16):
    entries = deviation * jax.random.normal(stream_key, dims, jnp.float32)
    if cuts:
        entries = entries * block_levels(stream_key, dims, cuts, -0.22, 0.18)
    return jnp.clip(entries, -bound, bound).astype(held_as)


def setup_inputs(seed: int = 0) -> dict:
    seeds = jax.random.split(jax.random.key(seed), 6)
    return {
        "amplitudes": bell_draw(seeds[0], (NO, NO, NV, NV), 1.0, 6.0, ((0, 8), (2, 4)), jnp.float32),
        "integrals": bell_draw(seeds[1], (W, W, NV, NV), (NV * NV) ** -0.5, 0.015625, ((0, 8), (2, 4)), jnp.float32),
        "rest": bell_draw(seeds[2], (NO, NO, W, W), 1.0, 6.0, ((0, 4), (2, 8)), jnp.float32),
        "occ_energy": jnp.clip(jax.random.uniform(seeds[3], (NO,), jnp.float32, -2.0, -0.5), -2.0, -0.5),
        "vir_energy": jnp.clip(jax.random.uniform(seeds[4], (W,), jnp.float32, 0.5, 3.0), 0.5, 3.0),
    }


def reference(amplitudes, integrals, rest, occ_energy, vir_energy):
    flattened = amplitudes.reshape(NO * NO, NV * NV)

    def one_virtual(integral_block):
        return jnp.dot(flattened, integral_block.reshape(W, NV * NV).T, precision=lax.Precision.HIGHEST, preferred_element_type=jnp.float32)

    stacked = lax.map(one_virtual, integrals)
    ladder = jnp.transpose(stacked, (1, 0, 2)).reshape(NO, NO, W, W)
    mirror = jnp.transpose(ladder, (1, 0, 3, 2))
    denominator = vir_energy[None, None, :, None] + vir_energy[None, None, None, :] - occ_energy[:, None, None, None] - occ_energy[None, :, None, None]
    return (ladder + mirror + rest) / denominator
```

```python
import functools

import jax
import jax.numpy as jnp
from jax import lax
from jax.experimental import pallas as pl
from jax.experimental.pallas import tpu as pltpu
from jax.sharding import PartitionSpec as P

MESH = pl.DeviceIdType.MESH
LANES = 128
LAG = 2


def chunk_of(count):
    return max(k for k in range(1, 11) if count % k == 0)


def split(x):
    high = x.astype(jnp.bfloat16)
    return high, (x - high.astype(jnp.float32)).astype(jnp.bfloat16)


def ring_kernel(n, cc, t_ref, ttail_ref, v_ref, vtail_ref, out_ref, held, vbuf, acc,
                load_sem, v_sem, send_sem, recv_sem):
    occ_rows, c_count, j_count, _ = t_ref.shape
    a_count, _, b_count, _ = v_ref.shape
    tail_tiles = ttail_ref.shape[0]
    full = v_ref.shape[3] // LANES
    rows = n * occ_rows * j_count
    cols = a_count * b_count
    mains = c_count // cc
    chunks = mains + 1

    row = lax.axis_index("row")
    half = n // 2

    def row_at(position):
        upper = lax.div(position, half)
        return (1 - upper) * (2 * position) + upper * (2 * (n - 1 - position) + 1)

    odd = lax.rem(row, 2)
    place = (1 - odd) * lax.div(row, 2) + odd * (n - 1 - lax.div(row, 2))
    source = {step: row_at(lax.rem(place + step + n, n)) for step in range(-half, half + 1)}

    def tiles(q):
        if q < mains:
            return pl.ds(q * full * cc, full * cc)
        return pl.ds(mains * full * cc, tail_tiles)

    def own_loads(q):
        if q == mains:
            return [pltpu.make_async_copy(ttail_ref, held.at[row, tiles(q)], load_sem.at[q])]
        return [
            pltpu.make_async_copy(
                t_ref.at[i, pl.ds(q * cc, cc), :, pl.ds(part * LANES, LANES)],
                held.at[row, pl.ds(q * full * cc + part * cc, cc), pl.ds(i * j_count, j_count), :],
                load_sem.at[q],
            )
            for i in range(occ_rows)
            for part in range(full)
        ]

    def v_load(q):
        return pltpu.make_async_copy(v_ref.at[:, pl.ds(q * cc, cc)], vbuf.at[q % 2], v_sem.at[q % 2])

    def hops(q, way):
        return half if (q + way) % 2 == 0 else n - 1 - half

    def send(q, step, way):
        sign = 1 if way == 0 else -1
        data = held.at[source[-sign * (step - 1)], tiles(q)]
        return pltpu.make_async_remote_copy(
            src_ref=data, dst_ref=data,
            send_sem=send_sem.at[q, step - 1, way], recv_sem=recv_sem.at[q, step - 1, way],
            device_id={"row": source[sign]}, device_id_type=MESH,
        )

    def arrival(q, step, way):
        sign = 1 if way == 0 else -1
        data = held.at[source[-sign * step], tiles(q)]
        return pltpu.make_async_remote_copy(
            src_ref=data, dst_ref=data,
            send_sem=send_sem.at[q, step - 1, way], recv_sem=recv_sem.at[q, step - 1, way],
            device_id={"row": source[sign]}, device_id_type=MESH,
        )

    def add_product(t, v):
        t_high, t_low = split(t)
        v_high, v_low = split(v)
        dims = (((1,), (1,)), ((), ()))
        both = lax.dot_general(t_high, jnp.concatenate([v_high, v_low], axis=0), dims,
                               preferred_element_type=jnp.float32)
        rest = lax.dot_general(t_low, v_high, dims, preferred_element_type=jnp.float32)
        acc[...] += both[:, :cols] + both[:, cols:] + rest

    def compute(q):
        if q == mains:
            @pl.loop(0, tail_tiles)
            def _(k):
                add_product(held[:, mains * full * cc + k].reshape(rows, LANES), vtail_ref[k])
            return
        v_load(q).wait()

        @pl.loop(0, cc)
        def _(k):
            t = jnp.concatenate(
                [held[:, q * full * cc + part * cc + k].reshape(rows, LANES) for part in range(full)], axis=1)
            v = vbuf[q % 2, :, k, :, : full * LANES].reshape(cols, full * LANES)
            add_product(t, v)
        if q + 2 < mains:
            v_load(q + 2).start()

    for q in range(chunks):
        for copy in own_loads(q):
            copy.start()
    for q in range(min(2, mains)):
        v_load(q).start()
    acc[...] = jnp.zeros_like(acc)

    barrier = pltpu.get_barrier_semaphore()
    for step in (-1, 1):
        pl.semaphore_signal(barrier, inc=1, device_id={"row": source[step]}, device_id_type=MESH)
    pl.semaphore_wait(barrier, 2)

    for turn in range(chunks + LAG * half):
        for step in range(1, half + 2):
            q = turn - LAG * (step - 1)
            if not 0 <= q < chunks:
                continue
            if step == 1:
                whole = held.at[row, tiles(q)]
                pltpu.make_async_copy(whole, whole, load_sem.at[q]).wait()
            for way in range(2):
                if step > 1 and step - 1 <= hops(q, way):
                    arrival(q, step - 1, way).wait_recv()
                if step <= hops(q, way):
                    send(q, step, way).start()
            if step == half + 1:
                compute(q)
    for q in range(chunks):
        for way in range(2):
            for step in range(1, hops(q, way) + 1):
                send(q, step, way).wait_send()
    out_ref[...] = acc[...]


def packed_tail(x, start):
    c_count, rows, d_count = x.shape
    width = d_count - start
    per = LANES // width
    groups = -(-c_count // per)
    cut = jnp.pad(x[:, :, start:], ((0, groups * per - c_count), (0, 0), (0, 0)))
    cut = cut.reshape(groups, per, rows, width).transpose(0, 2, 1, 3).reshape(groups, rows, per * width)
    return jnp.pad(cut, ((0, 0), (0, 0), (0, LANES - per * width)))


def partial_ladder(n, amplitudes, integrals):
    occ_rows, j_count, c_count, d_count = amplitudes.shape
    a_count, b_count = integrals.shape[:2]
    full = d_count // LANES
    t = jnp.transpose(amplitudes, (0, 2, 1, 3))
    v = jnp.transpose(integrals, (0, 2, 1, 3))
    t_tail = packed_tail(
        jnp.transpose(t[..., full * LANES:], (1, 0, 2, 3)).reshape(c_count, occ_rows * j_count, -1), 0)
    v_tail = packed_tail(
        jnp.transpose(v[..., full * LANES:], (1, 0, 2, 3)).reshape(c_count, a_count * b_count, -1), 0)
    cc = chunk_of(c_count)
    chunks = c_count // cc + 1
    tiles = c_count * full + t_tail.shape[0]
    rows, cols = n * occ_rows * j_count, a_count * b_count
    half = n // 2
    return pl.pallas_call(
        functools.partial(ring_kernel, n, cc),
        out_shape=jax.ShapeDtypeStruct((rows, cols), jnp.float32),
        in_specs=[pl.BlockSpec(memory_space=pl.ANY)] * 3 + [pl.BlockSpec(memory_space=pltpu.VMEM)],
        out_specs=pl.BlockSpec(memory_space=pltpu.VMEM),
        scratch_shapes=[
            pltpu.VMEM((n, tiles, occ_rows * j_count, LANES), jnp.float32),
            pltpu.VMEM((2, a_count, cc, b_count, d_count), jnp.float32),
            pltpu.VMEM((rows, cols), jnp.float32),
            pltpu.SemaphoreType.DMA((chunks,)),
            pltpu.SemaphoreType.DMA((2,)),
            pltpu.SemaphoreType.DMA((chunks, half, 2)),
            pltpu.SemaphoreType.DMA((chunks, half, 2)),
        ],
        compiler_params=pltpu.CompilerParams(
            collective_id=0, has_side_effects=True, vmem_limit_bytes=58 * 2**20),
        cost_estimate=pl.CostEstimate(
            flops=6 * rows * cols * c_count * d_count,
            bytes_accessed=4 * c_count * d_count * (rows + cols), transcendentals=0),
    )(t, t_tail, v, v_tail)


def on_device(n, amplitudes, integrals, rest, occ_energy, vir_energy):
    row_index = lax.axis_index("row")
    col_index = lax.axis_index("col")
    a_count = integrals.shape[0]
    b_count = integrals.shape[1]
    occupied = amplitudes.shape[1]
    partial_value = partial_ladder(n, amplitudes, integrals).reshape(
        n * amplitudes.shape[0], occupied, a_count, b_count)
    summed = lax.psum_scatter(partial_value, "col", scatter_dimension=0, tiled=True)
    moved = lax.all_to_all(
        lax.all_to_all(summed, "row", split_axis=3, concat_axis=2, tiled=True),
        "col",
        split_axis=1,
        concat_axis=0,
        tiled=True,
    )
    combined = summed + jnp.transpose(moved, (1, 0, 3, 2))
    i_count = combined.shape[0]
    occ_local = lax.dynamic_slice_in_dim(occ_energy, col_index * i_count, i_count, 0)
    vir_local = lax.dynamic_slice_in_dim(vir_energy, row_index * a_count, a_count, 0)
    denominator = (
        vir_local[None, None, :, None]
        + vir_energy[None, None, None, :]
        - occ_local[:, None, None, None]
        - occ_energy[None, :, None, None]
    )
    return (combined + rest) / denominator


def solution(mesh):
    in_specs = (
        P("row", None, "col", None),
        P("row", None, "col", None),
        P("col", None, "row", None),
        P(),
        P(),
    )
    out_specs = P("col", None, "row", None)
    return jax.shard_map(
        functools.partial(on_device, mesh.shape["row"]), mesh=mesh, in_specs=in_specs, out_specs=out_specs,
        check_vma=False
    )
```

```python
import functools

import jax
import jax.numpy as jnp
from jax import lax
from jax.experimental import pallas as pl
from jax.experimental.pallas import tpu as pltpu
from jax.sharding import PartitionSpec as P

MESH = pl.DeviceIdType.MESH
LANES = 128
LAG = 2


def chunk_of(count, most):
    return max(k for k in range(1, most + 1) if count % k == 0)


def split(x):
    high = x.astype(jnp.bfloat16)
    return high, (x - high.astype(jnp.float32)).astype(jnp.bfloat16)


def ring_kernel(n, cc, t_ref, ttail_ref, v_ref, vtail_ref, out_ref, held, vbuf, acc,
                load_sem, v_sem, send_sem, recv_sem):
    occ_rows, c_count, j_count, _ = t_ref.shape
    a_count, _, b_count, _ = v_ref.shape
    tail_tiles = ttail_ref.shape[0]
    full = v_ref.shape[3] // LANES
    rows = n * occ_rows * j_count
    cols = a_count * b_count
    mains = c_count // cc
    chunks = mains + 1

    row = lax.axis_index("row")
    half = n // 2

    def row_at(position):
        upper = lax.div(position, half)
        return (1 - upper) * (2 * position) + upper * (2 * (n - 1 - position) + 1)

    odd = lax.rem(row, 2)
    place = (1 - odd) * lax.div(row, 2) + odd * (n - 1 - lax.div(row, 2))
    source = {step: row_at(lax.rem(place + step + n, n)) for step in range(-half, half + 1)}

    def tiles(q):
        if q < mains:
            return pl.ds(q * full * cc, full * cc)
        return pl.ds(mains * full * cc, tail_tiles)

    def own_loads(q):
        if q == mains:
            return [pltpu.make_async_copy(ttail_ref, held.at[row, tiles(q)], load_sem.at[q])]
        return [
            pltpu.make_async_copy(
                t_ref.at[i, pl.ds(q * cc, cc), :, pl.ds(part * LANES, LANES)],
                held.at[row, pl.ds(q * full * cc + part * cc, cc), pl.ds(i * j_count, j_count), :],
                load_sem.at[q],
            )
            for i in range(occ_rows)
            for part in range(full)
        ]

    def v_load(q):
        return pltpu.make_async_copy(v_ref.at[:, pl.ds(q * cc, cc)], vbuf.at[q % 2], v_sem.at[q % 2])

    def hops(q, way):
        return half if (q + way) % 2 == 0 else n - 1 - half

    def send(q, step, way):
        sign = 1 if way == 0 else -1
        data = held.at[source[-sign * (step - 1)], tiles(q)]
        return pltpu.make_async_remote_copy(
            src_ref=data, dst_ref=data,
            send_sem=send_sem.at[q, step - 1, way], recv_sem=recv_sem.at[q, step - 1, way],
            device_id={"row": source[sign]}, device_id_type=MESH,
        )

    def arrival(q, step, way):
        sign = 1 if way == 0 else -1
        data = held.at[source[-sign * step], tiles(q)]
        return pltpu.make_async_remote_copy(
            src_ref=data, dst_ref=data,
            send_sem=send_sem.at[q, step - 1, way], recv_sem=recv_sem.at[q, step - 1, way],
            device_id={"row": source[sign]}, device_id_type=MESH,
        )

    def add_product(t, v):
        t_high, t_low = split(t)
        v_high, v_low = split(v)
        dims = (((1,), (1,)), ((), ()))
        both = lax.dot_general(t_high, jnp.concatenate([v_high, v_low], axis=0), dims,
                               preferred_element_type=jnp.float32)
        rest = lax.dot_general(t_low, v_high, dims, preferred_element_type=jnp.float32)
        acc[...] += both[:, :cols] + both[:, cols:] + rest

    def compute(q):
        if q == mains:
            @pl.loop(0, tail_tiles)
            def _(k):
                add_product(held[:, mains * full * cc + k].reshape(rows, LANES), vtail_ref[k])
            return
        v_load(q).wait()

        @pl.loop(0, cc)
        def _(k):
            t = jnp.concatenate(
                [held[:, q * full * cc + part * cc + k].reshape(rows, LANES) for part in range(full)], axis=1)
            v = vbuf[q % 2, :, k, :, : full * LANES].reshape(cols, full * LANES)
            add_product(t, v)
        if q + 2 < mains:
            v_load(q + 2).start()

    for q in range(chunks):
        for copy in own_loads(q):
            copy.start()
    for q in range(min(2, mains)):
        v_load(q).start()
    acc[...] = jnp.zeros_like(acc)

    barrier = pltpu.get_barrier_semaphore()
    for step in (-1, 1):
        pl.semaphore_signal(barrier, inc=1, device_id={"row": source[step]}, device_id_type=MESH)
    pl.semaphore_wait(barrier, 2)

    for turn in range(chunks + LAG * half):
        for step in range(1, half + 2):
            q = turn - LAG * (step - 1)
            if not 0 <= q < chunks:
                continue
            if step == 1:
                whole = held.at[row, tiles(q)]
                pltpu.make_async_copy(whole, whole, load_sem.at[q]).wait()
            for way in range(2):
                if step > 1 and step - 1 <= hops(q, way):
                    arrival(q, step - 1, way).wait_recv()
                if step <= hops(q, way):
                    send(q, step, way).start()
            if step == half + 1:
                compute(q)
    for q in range(chunks):
        for way in range(2):
            for step in range(1, hops(q, way) + 1):
                send(q, step, way).wait_send()
    out_ref[...] = acc[...]


def packed_tail(x, start):
    c_count, rows, d_count = x.shape
    width = d_count - start
    per = LANES // width
    groups = -(-c_count // per)
    cut = jnp.pad(x[:, :, start:], ((0, groups * per - c_count), (0, 0), (0, 0)))
    cut = cut.reshape(groups, per, rows, width).transpose(0, 2, 1, 3).reshape(groups, rows, per * width)
    return jnp.pad(cut, ((0, 0), (0, 0), (0, LANES - per * width)))


def pair_kernel(n, cc, away, t_ref, ttail_ref, v_ref, vtail_ref, out_ref, held, stage, vbuf, far, away_v, vtail, far_tail,
                acc, acc_away, got_away, got_pair, load_sem, stage_sem, v_sem, vt_sem, tp_send, tp_recv, vp_send,
                vp_recv, z_send, z_recv, a_send, a_recv, back_sem, pair_sem):
    occ_rows, c_count, j_count, _ = t_ref.shape
    a_count, _, b_count, d_count = v_ref.shape
    tail_tiles = ttail_ref.shape[1]
    full = d_count // LANES
    width = full * LANES
    rows = n * occ_rows * j_count
    cols = a_count * b_count
    own_c = c_count // 2
    mains = own_c // cc
    chunks = mains + 1
    line = n // 2

    row = lax.axis_index("row")
    z, y = lax.div(row, 2), lax.rem(row, 2)
    pair = 2 * z + 1 - y
    low_end, high_end = z == 0, z == line - 1
    end = jnp.logical_or(low_end, high_end)
    low_help, high_help = z == 1, z == line - 2
    helper = jnp.logical_or(low_help, high_help)

    def to(target):
        return {"row": target}

    def tiles(q):
        if q < mains:
            return pl.ds(q * full * cc, full * cc)
        return pl.ds(mains * full * cc, tail_tiles)

    def t_loads(q, side, target, sem):
        if q == mains:
            return [pltpu.make_async_copy(ttail_ref.at[side], target.at[tiles(q)], sem.at[q])]
        return [
            pltpu.make_async_copy(
                t_ref.at[i, pl.ds(side * own_c + q * cc, cc), :, pl.ds(part * LANES, LANES)],
                target.at[pl.ds(q * full * cc + part * cc, cc), pl.ds(i * j_count, j_count), :],
                sem.at[q],
            )
            for i in range(occ_rows)
            for part in range(full)
        ]

    def whole_wait(data, sem):
        pltpu.make_async_copy(data, data, sem).wait()

    def v_piece(q, side):
        return v_ref.at[:, pl.ds(side * own_c + q * cc, cc), :, pl.ds(0, width)]

    def v_load(q):
        return pltpu.make_async_copy(v_piece(q, y), vbuf.at[q % 2], v_sem.at[q % 2])

    own_vtail = pltpu.make_async_copy(vtail_ref.at[y], vtail, vt_sem)

    def remote(src, dst, send, recv, target):
        return pltpu.make_async_remote_copy(src_ref=src, dst_ref=dst, send_sem=send, recv_sem=recv,
                                            device_id=to(target), device_id_type=MESH)

    def t_to_pair(q):
        return remote(stage.at[tiles(q)], held.at[row, tiles(q)], tp_send.at[q], tp_recv.at[q], pair)

    def t_from_pair(q):
        data = held.at[pair, tiles(q)]
        return remote(data, data, tp_send.at[q], tp_recv.at[q], pair)

    def v_to_pair(q):
        if q == mains:
            return remote(vtail_ref.at[1 - y], far_tail, vp_send.at[q], vp_recv.at[q], pair)
        return remote(v_piece(q, 1 - y), far.at[q], vp_send.at[q], vp_recv.at[q], pair)

    def along(q, step, way, arriving):
        sign = 1 - 2 * way
        start = z - sign * (step if arriving else step - 1)
        data = held.at[pl.ds(2 * start, 2), tiles(q)]
        return remote(data, data, z_send.at[q, step - 1, way], z_recv.at[q, step - 1, way], row + 2 * sign)

    def sends(q, step, way):
        last = line - 2 if q < away else line - 1
        if way == 0:
            return jnp.logical_and(z - (step - 1) >= 0, z + 1 <= last)
        return jnp.logical_and(z + (step - 1) <= line - 1, z - 1 >= line - 1 - last)

    def arrives(q, step, way):
        last = line - 2 if q < away else line - 1
        if way == 0:
            return jnp.logical_and(z - step >= 0, z <= last)
        return jnp.logical_and(z + step <= line - 1, z >= line - 1 - last)

    def v_away(q, block, inner):
        src = v_piece(q, y) if block == 0 else far.at[q]
        return remote(src, away_v.at[q, block], a_send.at[q, block], a_recv.at[q, block], inner)

    def v_arrived(q, block):
        data = away_v.at[q, block]
        return remote(data, data, a_send.at[q, block], a_recv.at[q, block], pair)

    def back(outer):
        return remote(acc_away, got_away, back_sem.at[0], back_sem.at[1], outer)

    def exchange():
        return remote(acc.at[1], got_pair, pair_sem.at[0], pair_sem.at[1], pair)

    def on_ends(f):
        pl.when(low_end)(lambda: f(row + 2))
        pl.when(high_end)(lambda: f(row - 2))

    def on_helpers(f):
        pl.when(low_help)(lambda: f(row - 2))
        pl.when(high_help)(lambda: f(row + 2))

    def add_product(into, t, v_own, v_far):
        t_high, t_low = split(t)
        v_high, v_low = split(jnp.concatenate([v_own, v_far], axis=0))
        dims = (((1,), (1,)), ((), ()))
        both = lax.dot_general(t_high, jnp.concatenate([v_high, v_low], axis=0), dims,
                               preferred_element_type=jnp.float32)
        rest = lax.dot_general(t_low, v_high, dims, preferred_element_type=jnp.float32)
        total = both[:, : 2 * cols] + both[:, 2 * cols:] + rest
        into[0] += total[:, :cols]
        into[1] += total[:, cols:]

    def t_of(q, k):
        return jnp.concatenate(
            [held[:, q * full * cc + part * cc + k].reshape(rows, LANES) for part in range(full)], axis=1)

    def compute(q):
        v_to_pair(q).wait_recv()
        if q == mains:
            own_vtail.wait()

            @pl.loop(0, tail_tiles)
            def _(k):
                add_product(acc, held[:, mains * full * cc + k].reshape(rows, LANES), vtail[k], far_tail[k])
            return
        v_load(q).wait()
        if q < away:
            on_ends(lambda inner: v_away(q, 1, inner).start())

        def product():
            @pl.loop(0, cc)
            def _(k):
                add_product(acc, t_of(q, k), vbuf[q % 2, :, k].reshape(cols, width), far[q, :, k].reshape(cols, width))

        if q < away:
            pl.when(jnp.logical_not(end))(product)
        else:
            product()
        if q + 2 < mains:
            v_load(q + 2).start()

    def compute_away():
        for q in range(away):
            for block in range(2):
                v_arrived(q, block).wait_recv()

            @pl.loop(0, cc)
            def _(k):
                add_product(acc_away, t_of(q, k), away_v[q, 0, :, k].reshape(cols, width),
                            away_v[q, 1, :, k].reshape(cols, width))

    for q in range(chunks):
        for copy in t_loads(q, 1 - y, stage, stage_sem) + t_loads(q, y, held.at[row], load_sem):
            copy.start()
    for q in range(min(2, mains)):
        v_load(q).start()
    own_vtail.start()
    acc[...] = jnp.zeros_like(acc)
    acc_away[...] = jnp.zeros_like(acc_away)

    barrier = pltpu.get_barrier_semaphore()
    pl.semaphore_signal(barrier, inc=1, device_id=to(pair), device_id_type=MESH)

    @pl.when(z > 0)
    def _():
        pl.semaphore_signal(barrier, inc=1, device_id=to(row - 2), device_id_type=MESH)

    @pl.when(z < line - 1)
    def _():
        pl.semaphore_signal(barrier, inc=1, device_id=to(row + 2), device_id_type=MESH)

    pl.semaphore_wait(barrier, 1 + jnp.minimum(z, 1) + jnp.minimum(line - 1 - z, 1))

    for q in range(chunks):
        whole_wait(stage.at[tiles(q)], stage_sem.at[q])
        t_to_pair(q).start()
    for q in range(away):
        on_ends(lambda inner, q=q: v_away(q, 0, inner).start())

    help_turn = away - 1 + LAG * (line - 1) + 4
    turns = chunks + LAG * (line - 1)
    for turn in range(turns):
        for q in ([0, 1, 2] if turn == 0 else [turn + 2]):
            if q < chunks:
                v_to_pair(q).start()
        for step in range(1, line + 1):
            q = turn - LAG * (step - 1)
            if not 0 <= q < chunks:
                continue
            if step == 1:
                whole_wait(held.at[row, tiles(q)], load_sem.at[q])
                t_from_pair(q).wait_recv()
            for way in range(2):
                if step > 1:
                    @pl.when(arrives(q, step - 1, way))
                    def _():
                        along(q, step - 1, way, True).wait_recv()
                if step < line:
                    @pl.when(sends(q, step, way))
                    def _():
                        along(q, step, way, False).start()
            if step == line:
                compute(q)
        if away and turn == min(help_turn, turns - 1):
            pl.when(helper)(compute_away)
            on_helpers(lambda outer: back(outer).start())

    if away:
        @pl.when(end)
        def _():
            back(pair).wait_recv()
            acc[...] += got_away[...]

    exchange().start()
    for q in range(chunks):
        t_to_pair(q).wait_send()
        v_to_pair(q).wait_send()
        for way in range(2):
            for step in range(1, line):
                @pl.when(sends(q, step, way))
                def _():
                    along(q, step, way, False).wait_send()
    if away:
        for q in range(away):
            for block in range(2):
                on_ends(lambda inner, q=q, block=block: v_away(q, block, inner).wait_send())
        on_helpers(lambda outer: back(outer).wait_send())
    exchange().wait()
    out_ref[...] = acc[0] + got_pair[...]


def pair_ladder(n, amplitudes, integrals):
    occ_rows, j_count, c_count, d_count = amplitudes.shape
    a_count, b_count = integrals.shape[:2]
    full = d_count // LANES
    own_c = c_count // 2
    t = jnp.transpose(amplitudes, (0, 2, 1, 3))
    v = jnp.transpose(integrals, (0, 2, 1, 3))

    def tails(x):
        cut = jnp.transpose(x[..., full * LANES:], (1, 0, 2, 3)).reshape(2, own_c, -1, d_count - full * LANES)
        return jax.vmap(lambda part: packed_tail(part, 0))(cut)

    t_tail, v_tail = tails(t), tails(v)
    cc = chunk_of(own_c, 5)
    mains = own_c // cc
    away = mains // 5
    chunks, line = mains + 1, n // 2
    tail_tiles = t_tail.shape[1]
    held_rows = occ_rows * j_count
    tiles = own_c * full + tail_tiles
    rows, cols = n * held_rows, a_count * b_count
    dma = pltpu.SemaphoreType.DMA
    return pl.pallas_call(
        functools.partial(pair_kernel, n, cc, away),
        out_shape=jax.ShapeDtypeStruct((rows, cols), jnp.float32),
        in_specs=[pl.BlockSpec(memory_space=pl.ANY)] * 4,
        out_specs=pl.BlockSpec(memory_space=pltpu.VMEM),
        scratch_shapes=[
            pltpu.VMEM((n, tiles, held_rows, LANES), jnp.float32),
            pltpu.VMEM((tiles, held_rows, LANES), jnp.float32),
            pltpu.VMEM((2, a_count, cc, b_count, full * LANES), jnp.float32),
            pltpu.VMEM((mains, a_count, cc, b_count, full * LANES), jnp.float32),
            pltpu.VMEM((max(away, 1), 2, a_count, cc, b_count, full * LANES), jnp.float32),
            pltpu.VMEM((tail_tiles, cols, LANES), jnp.float32),
            pltpu.VMEM((tail_tiles, cols, LANES), jnp.float32),
            pltpu.VMEM((2, rows, cols), jnp.float32),
            pltpu.VMEM((2, rows, cols), jnp.float32),
            pltpu.VMEM((2, rows, cols), jnp.float32),
            pltpu.VMEM((rows, cols), jnp.float32),
            dma((chunks,)), dma((chunks,)), dma((2,)), dma(()), dma((chunks,)), dma((chunks,)), dma((chunks,)),
            dma((chunks,)), dma((chunks, line - 1, 2)), dma((chunks, line - 1, 2)), dma((max(away, 1), 2)),
            dma((max(away, 1), 2)), dma((2,)), dma((2,)),
        ],
        compiler_params=pltpu.CompilerParams(
            collective_id=1, has_side_effects=True, vmem_limit_bytes=58 * 2**20),
        cost_estimate=pl.CostEstimate(
            flops=6 * rows * cols * c_count * d_count,
            bytes_accessed=4 * c_count * d_count * (rows + cols), transcendentals=0),
    )(t, t_tail, v, v_tail)


def partial_ladder(n, amplitudes, integrals):
    occ_rows, j_count, c_count, d_count = amplitudes.shape
    a_count, b_count = integrals.shape[:2]
    full = d_count // LANES
    t = jnp.transpose(amplitudes, (0, 2, 1, 3))
    v = jnp.transpose(integrals, (0, 2, 1, 3))
    t_tail = packed_tail(
        jnp.transpose(t[..., full * LANES:], (1, 0, 2, 3)).reshape(c_count, occ_rows * j_count, -1), 0)
    v_tail = packed_tail(
        jnp.transpose(v[..., full * LANES:], (1, 0, 2, 3)).reshape(c_count, a_count * b_count, -1), 0)
    cc = chunk_of(c_count, 10)
    chunks = c_count // cc + 1
    tiles = c_count * full + t_tail.shape[0]
    rows, cols = n * occ_rows * j_count, a_count * b_count
    half = n // 2
    return pl.pallas_call(
        functools.partial(ring_kernel, n, cc),
        out_shape=jax.ShapeDtypeStruct((rows, cols), jnp.float32),
        in_specs=[pl.BlockSpec(memory_space=pl.ANY)] * 3 + [pl.BlockSpec(memory_space=pltpu.VMEM)],
        out_specs=pl.BlockSpec(memory_space=pltpu.VMEM),
        scratch_shapes=[
            pltpu.VMEM((n, tiles, occ_rows * j_count, LANES), jnp.float32),
            pltpu.VMEM((2, a_count, cc, b_count, d_count), jnp.float32),
            pltpu.VMEM((rows, cols), jnp.float32),
            pltpu.SemaphoreType.DMA((chunks,)),
            pltpu.SemaphoreType.DMA((2,)),
            pltpu.SemaphoreType.DMA((chunks, half, 2)),
            pltpu.SemaphoreType.DMA((chunks, half, 2)),
        ],
        compiler_params=pltpu.CompilerParams(
            collective_id=0, has_side_effects=True, vmem_limit_bytes=58 * 2**20),
        cost_estimate=pl.CostEstimate(
            flops=6 * rows * cols * c_count * d_count,
            bytes_accessed=4 * c_count * d_count * (rows + cols), transcendentals=0),
    )(t, t_tail, v, v_tail)


def on_device(n, amplitudes, integrals, rest, occ_energy, vir_energy):
    row_index = lax.axis_index("row")
    col_index = lax.axis_index("col")
    a_count = integrals.shape[0]
    b_count = integrals.shape[1]
    occupied = amplitudes.shape[1]
    ladder = pair_ladder if n >= 8 and amplitudes.shape[2] % 2 == 0 else partial_ladder
    partial_value = ladder(n, amplitudes, integrals).reshape(
        n * amplitudes.shape[0], occupied, a_count, b_count)
    summed = lax.psum_scatter(partial_value, "col", scatter_dimension=0, tiled=True)
    moved = lax.all_to_all(
        lax.all_to_all(summed, "row", split_axis=3, concat_axis=2, tiled=True),
        "col",
        split_axis=1,
        concat_axis=0,
        tiled=True,
    )
    combined = summed + jnp.transpose(moved, (1, 0, 3, 2))
    i_count = combined.shape[0]
    occ_local = lax.dynamic_slice_in_dim(occ_energy, col_index * i_count, i_count, 0)
    vir_local = lax.dynamic_slice_in_dim(vir_energy, row_index * a_count, a_count, 0)
    denominator = (
        vir_local[None, None, :, None]
        + vir_energy[None, None, None, :]
        - occ_local[:, None, None, None]
        - occ_energy[None, :, None, None]
    )
    return (combined + rest) / denominator


def solution(mesh):
    in_specs = (
        P("row", None, "col", None),
        P("row", None, "col", None),
        P("col", None, "row", None),
        P(),
        P(),
    )
    out_specs = P("col", None, "row", None)
    return jax.shard_map(
        functools.partial(on_device, mesh.shape["row"]), mesh=mesh, in_specs=in_specs, out_specs=out_specs,
        check_vma=False
    )
```

```python
import functools

import jax
import jax.numpy as jnp
from jax import lax
from jax.experimental import pallas as pl
from jax.experimental.pallas import tpu as pltpu
from jax.sharding import PartitionSpec as P

MESH = pl.DeviceIdType.MESH
LANES = 128
LAG = 2


def chunk_of(count, most):
    return max(k for k in range(1, most + 1) if count % k == 0)


def split(x):
    high = x.astype(jnp.bfloat16)
    return high, (x - high.astype(jnp.float32)).astype(jnp.bfloat16)


def ring_kernel(n, cc, t_ref, ttail_ref, v_ref, vtail_ref, out_ref, held, vbuf, acc,
                load_sem, v_sem, send_sem, recv_sem):
    occ_rows, c_count, j_count, _ = t_ref.shape
    a_count, _, b_count, _ = v_ref.shape
    tail_tiles = ttail_ref.shape[0]
    full = v_ref.shape[3] // LANES
    rows = n * occ_rows * j_count
    cols = a_count * b_count
    mains = c_count // cc
    chunks = mains + 1

    row = lax.axis_index("row")
    half = n // 2

    def row_at(position):
        upper = lax.div(position, half)
        return (1 - upper) * (2 * position) + upper * (2 * (n - 1 - position) + 1)

    odd = lax.rem(row, 2)
    place = (1 - odd) * lax.div(row, 2) + odd * (n - 1 - lax.div(row, 2))
    source = {step: row_at(lax.rem(place + step + n, n)) for step in range(-half, half + 1)}

    def tiles(q):
        if q < mains:
            return pl.ds(q * full * cc, full * cc)
        return pl.ds(mains * full * cc, tail_tiles)

    def own_loads(q):
        if q == mains:
            return [pltpu.make_async_copy(ttail_ref, held.at[row, tiles(q)], load_sem.at[q])]
        return [
            pltpu.make_async_copy(
                t_ref.at[i, pl.ds(q * cc, cc), :, pl.ds(part * LANES, LANES)],
                held.at[row, pl.ds(q * full * cc + part * cc, cc), pl.ds(i * j_count, j_count), :],
                load_sem.at[q],
            )
            for i in range(occ_rows)
            for part in range(full)
        ]

    def v_load(q):
        return pltpu.make_async_copy(v_ref.at[:, pl.ds(q * cc, cc)], vbuf.at[q % 2], v_sem.at[q % 2])

    def hops(q, way):
        return half if (q + way) % 2 == 0 else n - 1 - half

    def send(q, step, way):
        sign = 1 if way == 0 else -1
        data = held.at[source[-sign * (step - 1)], tiles(q)]
        return pltpu.make_async_remote_copy(
            src_ref=data, dst_ref=data,
            send_sem=send_sem.at[q, step - 1, way], recv_sem=recv_sem.at[q, step - 1, way],
            device_id={"row": source[sign]}, device_id_type=MESH,
        )

    def arrival(q, step, way):
        sign = 1 if way == 0 else -1
        data = held.at[source[-sign * step], tiles(q)]
        return pltpu.make_async_remote_copy(
            src_ref=data, dst_ref=data,
            send_sem=send_sem.at[q, step - 1, way], recv_sem=recv_sem.at[q, step - 1, way],
            device_id={"row": source[sign]}, device_id_type=MESH,
        )

    def add_product(t, v):
        t_high, t_low = split(t)
        v_high, v_low = split(v)
        dims = (((1,), (1,)), ((), ()))
        both = lax.dot_general(t_high, jnp.concatenate([v_high, v_low], axis=0), dims,
                               preferred_element_type=jnp.float32)
        rest = lax.dot_general(t_low, v_high, dims, preferred_element_type=jnp.float32)
        acc[...] += both[:, :cols] + both[:, cols:] + rest

    def compute(q):
        if q == mains:
            @pl.loop(0, tail_tiles)
            def _(k):
                add_product(held[:, mains * full * cc + k].reshape(rows, LANES), vtail_ref[k])
            return
        v_load(q).wait()

        @pl.loop(0, cc)
        def _(k):
            t = jnp.concatenate(
                [held[:, q * full * cc + part * cc + k].reshape(rows, LANES) for part in range(full)], axis=1)
            v = vbuf[q % 2, :, k, :, : full * LANES].reshape(cols, full * LANES)
            add_product(t, v)
        if q + 2 < mains:
            v_load(q + 2).start()

    for q in range(chunks):
        for copy in own_loads(q):
            copy.start()
    for q in range(min(2, mains)):
        v_load(q).start()
    acc[...] = jnp.zeros_like(acc)

    barrier = pltpu.get_barrier_semaphore()
    for step in (-1, 1):
        pl.semaphore_signal(barrier, inc=1, device_id={"row": source[step]}, device_id_type=MESH)
    pl.semaphore_wait(barrier, 2)

    for turn in range(chunks + LAG * half):
        for step in range(1, half + 2):
            q = turn - LAG * (step - 1)
            if not 0 <= q < chunks:
                continue
            if step == 1:
                whole = held.at[row, tiles(q)]
                pltpu.make_async_copy(whole, whole, load_sem.at[q]).wait()
            for way in range(2):
                if step > 1 and step - 1 <= hops(q, way):
                    arrival(q, step - 1, way).wait_recv()
                if step <= hops(q, way):
                    send(q, step, way).start()
            if step == half + 1:
                compute(q)
    for q in range(chunks):
        for way in range(2):
            for step in range(1, hops(q, way) + 1):
                send(q, step, way).wait_send()
    out_ref[...] = acc[...]


def packed_tail(x, start):
    c_count, rows, d_count = x.shape
    width = d_count - start
    per = LANES // width
    groups = -(-c_count // per)
    cut = jnp.pad(x[:, :, start:], ((0, groups * per - c_count), (0, 0), (0, 0)))
    cut = cut.reshape(groups, per, rows, width).transpose(0, 2, 1, 3).reshape(groups, rows, per * width)
    return jnp.pad(cut, ((0, 0), (0, 0), (0, LANES - per * width)))


def pair_kernel(n, cc, away, t_ref, ttail_ref, v_ref, vtail_ref, out_ref, held, stage, vbuf, far, away_v, vtail, far_tail,
                acc, acc_away, got_away, got_pair, load_sem, stage_sem, v_sem, vt_sem, tp_send, tp_recv, vp_send,
                vp_recv, z_send, z_recv, a_send, a_recv, back_sem, pair_sem):
    occ_rows, c_count, j_count, _ = t_ref.shape
    a_count, _, b_count, d_count = v_ref.shape
    tail_tiles = ttail_ref.shape[1]
    full = d_count // LANES
    width = full * LANES
    rows = n * occ_rows * j_count
    cols = a_count * b_count
    own_c = c_count // 2
    mains = own_c // cc
    chunks = mains + 1
    line = n // 2

    row = lax.axis_index("row")
    z, y = lax.div(row, 2), lax.rem(row, 2)
    pair = 2 * z + 1 - y
    low_end, high_end = z == 0, z == line - 1
    end = jnp.logical_or(low_end, high_end)
    low_help, high_help = z == 1, z == line - 2
    helper = jnp.logical_or(low_help, high_help)

    def to(target):
        return {"row": target}

    def tiles(q):
        if q < mains:
            return pl.ds(q * full * cc, full * cc)
        return pl.ds(mains * full * cc, tail_tiles)

    def t_loads(q, side, target, sem):
        if q == mains:
            return [pltpu.make_async_copy(ttail_ref.at[side], target.at[tiles(q)], sem.at[q])]
        return [
            pltpu.make_async_copy(
                t_ref.at[i, pl.ds(side * own_c + q * cc, cc), :, pl.ds(part * LANES, LANES)],
                target.at[pl.ds(q * full * cc + part * cc, cc), pl.ds(i * j_count, j_count), :],
                sem.at[q],
            )
            for i in range(occ_rows)
            for part in range(full)
        ]

    def whole_wait(data, sem):
        pltpu.make_async_copy(data, data, sem).wait()

    def v_piece(q, side):
        return v_ref.at[:, pl.ds(side * own_c + q * cc, cc), :, pl.ds(0, width)]

    def v_load(q):
        return pltpu.make_async_copy(v_piece(q, y), vbuf.at[q % 2], v_sem.at[q % 2])

    own_vtail = pltpu.make_async_copy(vtail_ref.at[y], vtail, vt_sem)

    def remote(src, dst, send, recv, target):
        return pltpu.make_async_remote_copy(src_ref=src, dst_ref=dst, send_sem=send, recv_sem=recv,
                                            device_id=to(target), device_id_type=MESH)

    def t_to_pair(q):
        return remote(stage.at[tiles(q)], held.at[row, tiles(q)], tp_send.at[q], tp_recv.at[q], pair)

    def t_from_pair(q):
        data = held.at[pair, tiles(q)]
        return remote(data, data, tp_send.at[q], tp_recv.at[q], pair)

    def v_to_pair(q):
        if q == mains:
            return remote(vtail_ref.at[1 - y], far_tail, vp_send.at[q], vp_recv.at[q], pair)
        return remote(v_piece(q, 1 - y), far.at[q], vp_send.at[q], vp_recv.at[q], pair)

    def along(q, step, way, arriving):
        sign = 1 - 2 * way
        start = z - sign * (step if arriving else step - 1)
        data = held.at[pl.ds(2 * start, 2), tiles(q)]
        return remote(data, data, z_send.at[q, step - 1, way], z_recv.at[q, step - 1, way], row + 2 * sign)

    def sends(q, step, way):
        last = line - 2 if q < away else line - 1
        if way == 0:
            return jnp.logical_and(z - (step - 1) >= 0, z + 1 <= last)
        return jnp.logical_and(z + (step - 1) <= line - 1, z - 1 >= line - 1 - last)

    def arrives(q, step, way):
        last = line - 2 if q < away else line - 1
        if way == 0:
            return jnp.logical_and(z - step >= 0, z <= last)
        return jnp.logical_and(z + step <= line - 1, z >= line - 1 - last)

    def v_away(q, block, inner):
        src = v_piece(q, y) if block == 0 else far.at[q]
        return remote(src, away_v.at[q, block], a_send.at[q, block], a_recv.at[q, block], inner)

    def v_arrived(q, block):
        data = away_v.at[q, block]
        return remote(data, data, a_send.at[q, block], a_recv.at[q, block], pair)

    def back(outer):
        return remote(acc_away, got_away, back_sem.at[0], back_sem.at[1], outer)

    def exchange():
        return remote(acc.at[1], got_pair, pair_sem.at[0], pair_sem.at[1], pair)

    def on_ends(f):
        pl.when(low_end)(lambda: f(row + 2))
        pl.when(high_end)(lambda: f(row - 2))

    def on_helpers(f):
        pl.when(low_help)(lambda: f(row - 2))
        pl.when(high_help)(lambda: f(row + 2))

    def add_product(into, t, v_own, v_far):
        t_high, t_low = split(t)
        v_high, v_low = split(jnp.concatenate([v_own, v_far], axis=0))
        dims = (((1,), (1,)), ((), ()))
        both = lax.dot_general(t_high, jnp.concatenate([v_high, v_low], axis=0), dims,
                               preferred_element_type=jnp.float32)
        rest = lax.dot_general(t_low, v_high, dims, preferred_element_type=jnp.float32)
        total = both[:, : 2 * cols] + both[:, 2 * cols:] + rest
        into[0] += total[:, :cols]
        into[1] += total[:, cols:]

    def t_of(q, k):
        return jnp.concatenate(
            [held[:, q * full * cc + part * cc + k].reshape(rows, LANES) for part in range(full)], axis=1)

    def compute(q):
        v_to_pair(q).wait_recv()
        if q == mains:
            own_vtail.wait()

            @pl.loop(0, tail_tiles)
            def _(k):
                add_product(acc, held[:, mains * full * cc + k].reshape(rows, LANES), vtail[k], far_tail[k])
            return
        v_load(q).wait()
        if q < away:
            on_ends(lambda inner: v_away(q, 1, inner).start())

        def product():
            @pl.loop(0, cc)
            def _(k):
                add_product(acc, t_of(q, k), vbuf[q % 2, :, k].reshape(cols, width), far[q, :, k].reshape(cols, width))

        if q < away:
            pl.when(jnp.logical_not(end))(product)
        else:
            product()
        if q + 2 < mains:
            v_load(q + 2).start()

    def compute_away():
        for q in range(away):
            for block in range(2):
                v_arrived(q, block).wait_recv()

            @pl.loop(0, cc)
            def _(k):
                add_product(acc_away, t_of(q, k), away_v[q, 0, :, k].reshape(cols, width),
                            away_v[q, 1, :, k].reshape(cols, width))

    for q in range(chunks):
        for copy in t_loads(q, 1 - y, stage, stage_sem) + t_loads(q, y, held.at[row], load_sem):
            copy.start()
    for q in range(min(2, mains)):
        v_load(q).start()
    own_vtail.start()
    acc[...] = jnp.zeros_like(acc)
    acc_away[...] = jnp.zeros_like(acc_away)

    barrier = pltpu.get_barrier_semaphore()
    pl.semaphore_signal(barrier, inc=1, device_id=to(pair), device_id_type=MESH)

    @pl.when(z > 0)
    def _():
        pl.semaphore_signal(barrier, inc=1, device_id=to(row - 2), device_id_type=MESH)

    @pl.when(z < line - 1)
    def _():
        pl.semaphore_signal(barrier, inc=1, device_id=to(row + 2), device_id_type=MESH)

    pl.semaphore_wait(barrier, 1 + jnp.minimum(z, 1) + jnp.minimum(line - 1 - z, 1))

    for q in range(chunks):
        whole_wait(stage.at[tiles(q)], stage_sem.at[q])
        t_to_pair(q).start()
    for q in range(away):
        on_ends(lambda inner, q=q: v_away(q, 0, inner).start())

    help_turn = away - 1 + LAG * (line - 1) + 4
    turns = chunks + LAG * (line - 1)
    for turn in range(turns):
        for q in ([0, 1, 2] if turn == 0 else [turn + 2]):
            if q < chunks:
                v_to_pair(q).start()
        for step in range(1, line + 1):
            q = turn - LAG * (step - 1)
            if not 0 <= q < chunks:
                continue
            if step == 1:
                whole_wait(held.at[row, tiles(q)], load_sem.at[q])
                t_from_pair(q).wait_recv()
            for way in range(2):
                if step > 1:
                    @pl.when(arrives(q, step - 1, way))
                    def _():
                        along(q, step - 1, way, True).wait_recv()
                if step < line:
                    @pl.when(sends(q, step, way))
                    def _():
                        along(q, step, way, False).start()
            if step == line:
                compute(q)
        if away and turn == min(help_turn, turns - 1):
            pl.when(helper)(compute_away)
            on_helpers(lambda outer: back(outer).start())

    if away:
        @pl.when(end)
        def _():
            back(pair).wait_recv()
            acc[...] += got_away[...]

    exchange().start()
    for q in range(chunks):
        t_to_pair(q).wait_send()
        v_to_pair(q).wait_send()
        for way in range(2):
            for step in range(1, line):
                @pl.when(sends(q, step, way))
                def _():
                    along(q, step, way, False).wait_send()
    if away:
        for q in range(away):
            for block in range(2):
                on_ends(lambda inner, q=q, block=block: v_away(q, block, inner).wait_send())
        on_helpers(lambda outer: back(outer).wait_send())
    exchange().wait()
    out_ref[...] = acc[0] + got_pair[...]


def pair_ladder(n, amplitudes, integrals):
    occ_rows, j_count, c_count, d_count = amplitudes.shape
    a_count, b_count = integrals.shape[:2]
    full = d_count // LANES
    own_c = c_count // 2
    t = jnp.transpose(amplitudes, (0, 2, 1, 3))
    v = jnp.transpose(integrals, (0, 2, 1, 3))

    def tails(x):
        cut = jnp.transpose(x[..., full * LANES:], (1, 0, 2, 3)).reshape(2, own_c, -1, d_count - full * LANES)
        return jax.vmap(lambda part: packed_tail(part, 0))(cut)

    t_tail, v_tail = tails(t), tails(v)
    cc = chunk_of(own_c, 5)
    mains = own_c // cc
    away = mains // 5
    chunks, line = mains + 1, n // 2
    tail_tiles = t_tail.shape[1]
    held_rows = occ_rows * j_count
    tiles = own_c * full + tail_tiles
    rows, cols = n * held_rows, a_count * b_count
    dma = pltpu.SemaphoreType.DMA
    return pl.pallas_call(
        functools.partial(pair_kernel, n, cc, away),
        out_shape=jax.ShapeDtypeStruct((rows, cols), jnp.float32),
        in_specs=[pl.BlockSpec(memory_space=pl.ANY)] * 4,
        out_specs=pl.BlockSpec(memory_space=pltpu.VMEM),
        scratch_shapes=[
            pltpu.VMEM((n, tiles, held_rows, LANES), jnp.float32),
            pltpu.VMEM((tiles, held_rows, LANES), jnp.float32),
            pltpu.VMEM((2, a_count, cc, b_count, full * LANES), jnp.float32),
            pltpu.VMEM((mains, a_count, cc, b_count, full * LANES), jnp.float32),
            pltpu.VMEM((max(away, 1), 2, a_count, cc, b_count, full * LANES), jnp.float32),
            pltpu.VMEM((tail_tiles, cols, LANES), jnp.float32),
            pltpu.VMEM((tail_tiles, cols, LANES), jnp.float32),
            pltpu.VMEM((2, rows, cols), jnp.float32),
            pltpu.VMEM((2, rows, cols), jnp.float32),
            pltpu.VMEM((2, rows, cols), jnp.float32),
            pltpu.VMEM((rows, cols), jnp.float32),
            dma((chunks,)), dma((chunks,)), dma((2,)), dma(()), dma((chunks,)), dma((chunks,)), dma((chunks,)),
            dma((chunks,)), dma((chunks, line - 1, 2)), dma((chunks, line - 1, 2)), dma((max(away, 1), 2)),
            dma((max(away, 1), 2)), dma((2,)), dma((2,)),
        ],
        compiler_params=pltpu.CompilerParams(
            collective_id=1, has_side_effects=True, vmem_limit_bytes=58 * 2**20),
        cost_estimate=pl.CostEstimate(
            flops=6 * rows * cols * c_count * d_count,
            bytes_accessed=4 * c_count * d_count * (rows + cols), transcendentals=0),
    )(t, t_tail, v, v_tail)


def partial_ladder(n, amplitudes, integrals):
    occ_rows, j_count, c_count, d_count = amplitudes.shape
    a_count, b_count = integrals.shape[:2]
    full = d_count // LANES
    t = jnp.transpose(amplitudes, (0, 2, 1, 3))
    v = jnp.transpose(integrals, (0, 2, 1, 3))
    t_tail = packed_tail(
        jnp.transpose(t[..., full * LANES:], (1, 0, 2, 3)).reshape(c_count, occ_rows * j_count, -1), 0)
    v_tail = packed_tail(
        jnp.transpose(v[..., full * LANES:], (1, 0, 2, 3)).reshape(c_count, a_count * b_count, -1), 0)
    cc = chunk_of(c_count, 10)
    chunks = c_count // cc + 1
    tiles = c_count * full + t_tail.shape[0]
    rows, cols = n * occ_rows * j_count, a_count * b_count
    half = n // 2
    return pl.pallas_call(
        functools.partial(ring_kernel, n, cc),
        out_shape=jax.ShapeDtypeStruct((rows, cols), jnp.float32),
        in_specs=[pl.BlockSpec(memory_space=pl.ANY)] * 3 + [pl.BlockSpec(memory_space=pltpu.VMEM)],
        out_specs=pl.BlockSpec(memory_space=pltpu.VMEM),
        scratch_shapes=[
            pltpu.VMEM((n, tiles, occ_rows * j_count, LANES), jnp.float32),
            pltpu.VMEM((2, a_count, cc, b_count, d_count), jnp.float32),
            pltpu.VMEM((rows, cols), jnp.float32),
            pltpu.SemaphoreType.DMA((chunks,)),
            pltpu.SemaphoreType.DMA((2,)),
            pltpu.SemaphoreType.DMA((chunks, half, 2)),
            pltpu.SemaphoreType.DMA((chunks, half, 2)),
        ],
        compiler_params=pltpu.CompilerParams(
            collective_id=0, has_side_effects=True, vmem_limit_bytes=58 * 2**20),
        cost_estimate=pl.CostEstimate(
            flops=6 * rows * cols * c_count * d_count,
            bytes_accessed=4 * c_count * d_count * (rows + cols), transcendentals=0),
    )(t, t_tail, v, v_tail)


def mirrored(product, rows, cols, occupied, a_count, b_count):
    i_count = occupied // cols
    pieces = lax.all_to_all(product, "col", split_axis=0, concat_axis=0, tiled=True)
    summed = pieces.reshape(cols, -1, product.shape[1]).sum(axis=0)
    blocks = summed.reshape(i_count, cols, i_count, a_count, rows, a_count).transpose(4, 1, 2, 0, 5, 3)
    moved = lax.all_to_all(
        blocks.reshape(rows * cols, -1), ("row", "col"), split_axis=0, concat_axis=0, tiled=True)
    moved = moved.reshape(rows, cols, i_count, i_count, a_count, a_count).transpose(2, 1, 3, 4, 0, 5)
    shape = (i_count, occupied, a_count, b_count)
    return summed.reshape(shape) + moved.reshape(shape)


def on_device(n, amplitudes, integrals, rest, occ_energy, vir_energy):
    row_index = lax.axis_index("row")
    col_index = lax.axis_index("col")
    a_count = integrals.shape[0]
    b_count = integrals.shape[1]
    occupied = amplitudes.shape[1]
    ladder = pair_ladder if n >= 8 and amplitudes.shape[2] % 2 == 0 else partial_ladder
    product = ladder(n, amplitudes, integrals)
    combined = mirrored(product, n, lax.axis_size("col"), occupied, a_count, b_count)
    i_count = combined.shape[0]
    occ_local = lax.dynamic_slice_in_dim(occ_energy, col_index * i_count, i_count, 0)
    vir_local = lax.dynamic_slice_in_dim(vir_energy, row_index * a_count, a_count, 0)
    denominator = (
        vir_local[None, None, :, None]
        + vir_energy[None, None, None, :]
        - occ_local[:, None, None, None]
        - occ_energy[None, :, None, None]
    )
    return (combined + rest) / denominator


def solution(mesh):
    in_specs = (
        P("row", None, "col", None),
        P("row", None, "col", None),
        P("col", None, "row", None),
        P(),
        P(),
    )
    out_specs = P("col", None, "row", None)
    return jax.shard_map(
        functools.partial(on_device, mesh.shape["row"]), mesh=mesh, in_specs=in_specs, out_specs=out_specs,
        check_vma=False
    )
```
